32 devices in a mesh: branch: 4 (over z), mp: 2 (over x), dp: 4 (over y, core).
Axes of the slice: x: 2, y: 2, z: 4, core: 2. Of those that a mesh axis runs over, the one named last changes fastest.
Arguments:
- context: bfloat16 [2048, 4096], P(('branch', 'dp'), 'mp'), may hold values from -6 to 6
- residual: bfloat16 [2048, 4096], P(('branch', 'dp')), may hold values from -12 to 12
- attn_weight: bfloat16 [4, 4096, 4096], P('branch', 'mp', 'dp'), may hold values from -0.1875 to 0.1875
- norm_gain: bfloat16 [4096], replicated, may hold values from 0.099609375 to 1.8984375
- gate_weight: bfloat16 [4, 4096, 5504], P('branch', None, ('mp', 'dp')), may hold values from -0.09375 to 0.09375
- up_weight: bfloat16 [4, 4096, 5504], P('branch', None, ('mp', 'dp')), may hold values from -0.09375 to 0.09375
- down_weight: bfloat16 [4, 5504, 4096], P('branch', ('mp', 'dp')), may hold values from -0.078125 to 0.078125
- cotangent: bfloat16 [2048, 4096], P(('branch', 'dp')), may hold values from -0.796875 to 0.796875
- expert_ids: int32 [2048, 2], P(('branch', 'dp')), may hold values from 0 to 3, as said below
- gate_fixed: int32 [2048, 2], P(('branch', 'dp')), may hold values from 1 to 32767, as said below
Outputs:
- grad_gate: bfloat16 [4, 4096, 5504], P('branch', None, ('mp', 'dp'))
- grad_up: bfloat16 [4, 4096, 5504], P('branch', None, ('mp', 'dp'))
- grad_down: bfloat16 [4, 5504, 4096], P('branch', ('mp', 'dp'))
The draws below stay inside these ranges and needn't reach their ends.
Inputs may be any that keep to these rules, and one draw needn't show every extreme that they name: `expert_ids`: the two entries of a row differ; in every aligned block of 128 rows some expert is named by more than 80 choices. `gate_fixed`: the two entries of a row sum to 32768.
All inputs are finite; a program needn't handle non-finite values.
Results may differ from the reference program's by a relative error of at most 0.025.
Values may be sent and summed in bfloat16 or wider, within the bound.
No kernel may reach another device: no remote copies, remote signals or barrier semaphores. Data moves between devices by JAX's collectives and lax.ppermute only.
A program may use at most 128 MiB of HBM per device.

```python
import math
import jax
import jax.numpy as jnp
from jax import lax

D = 4096
FF = 5504
TOK_DEV = 128
BRANCHES = 4
EXPERTS = 4
TOKENS = 2048
CAP = 80
N_MP = 2


def shuffle_group(group_key):
    return jax.random.permutation(group_key, TOK_DEV)


def route_table(key):
    base_key = jax.random.fold_in(key, 17)
    key_hot, key_perm, key_first, key_second = jax.random.split(base_key, 4)
    groups = TOKENS // TOK_DEV
    hot_expert = jax.random.randint(key_hot, (), 0, EXPERTS)
    ranking = jax.vmap(shuffle_group)(jax.random.split(key_perm, groups))
    hot_count = min(TOK_DEV, CAP + CAP // 4)
    chosen = ranking < hot_count
    other_pick = (hot_expert + 1 + jax.random.randint(key_first, (groups, TOK_DEV), 0, EXPERTS - 1)) % EXPERTS
    first_pick = jnp.where(chosen, hot_expert, other_pick)
    second = (first_pick + 1 + jax.random.randint(key_second, (groups, TOK_DEV), 0, EXPERTS - 1)) % EXPERTS
    expert_table = jnp.stack([first_pick, second], axis=2).reshape(TOKENS, 2)
    return expert_table.astype(jnp.int32)


def draw_expert_ids(key, part):
    return route_table(key)


def draw_gate_fixed(key, part):
    first_part = jax.random.randint(jax.random.fold_in(key, 31), (TOKENS, 1), 1, 32768)
    return jnp.concatenate([first_part, 32768 - first_part], axis=1).astype(jnp.int32)


def draw_residual(key, part):
    key_base, key_rows, key_cols = jax.random.split(jax.random.fold_in(key, 23), 3)
    values = jax.random.normal(key_base, (TOKENS, D), jnp.float32)
    row_scale = jnp.exp(jax.random.uniform(key_rows, (TOKENS, 1), jnp.float32, math.log(0.3), math.log(3.0)))
    col_scale = jnp.exp(jax.random.uniform(key_cols, (1, D), jnp.float32, math.log(0.5), math.log(2.0)))
    values = values * row_scale * col_scale
    return jnp.clip(values, -12.0, 12.0).astype(jnp.bfloat16)


def levels(own_key, shape, cuts, least, largest):
    loudness = 1.0
    for dim, blocks in cuts:
        draws = jax.random.uniform(jax.random.fold_in(jax.random.fold_in(own_key, 6), dim), (blocks,), jnp.float32, least / len(cuts), largest / len(cuts))
        loudness = loudness * jnp.repeat(jnp.exp(draws), shape[dim] // blocks).reshape((-1,) + (1,) * (len(shape) - 1 - dim))
    return loudness


def noise(own_key, shape, width, most, shards=(), held_as=jnp.bfloat16):
    result = jax.random.normal(own_key, shape, jnp.float32) * width
    if len(shards) > 0:
        result = levels(own_key, shape, shards, -0.22, 0.18) * result
    return jnp.clip(result, min=-most, max=most).astype(held_as)


def setup_inputs(seed: int = 0) -> dict:
    key_of = jax.random.split(jax.random.key(seed), 11)
    context = noise(key_of[0], (TOKENS, D), 1.0, 6.0, ((0, 16), (1, 2)))
    residual = draw_residual(jax.random.fold_in(key_of[10], 71), 0)
    attn_weight = noise(key_of[2], (BRANCHES, D, D), (D // BRANCHES) ** -0.5, 0.1875, ((0, 4), (1, 2), (2, 4)))
    norm_gain = jnp.clip(1.0 + 0.18 * jax.random.normal(key_of[3], (D,), jnp.float32), 0.099609375, 1.8984375).astype(jnp.bfloat16)
    gate_weight = noise(key_of[4], (EXPERTS, D, FF), D ** -0.5, 0.09375, ((0, 4), (2, 8)))
    up_weight = noise(key_of[5], (EXPERTS, D, FF), D ** -0.5, 0.09375, ((0, 4), (2, 8)))
    down_weight = noise(key_of[6], (EXPERTS, FF, D), FF ** -0.5, 0.078125, ((0, 4), (1, 8)))
    cotangent = noise(key_of[7], (TOKENS, D), 0.1, 0.796875, ((0, 16),))
    expert_ids = draw_expert_ids(jax.random.fold_in(key_of[10], 71), 0)
    gate_fixed = draw_gate_fixed(jax.random.fold_in(key_of[10], 71), 0)
    return {"context": context, "residual": residual, "attn_weight": attn_weight, "norm_gain": norm_gain, "gate_weight": gate_weight, "up_weight": up_weight, "down_weight": down_weight, "cotangent": cotangent, "expert_ids": expert_ids, "gate_fixed": gate_fixed}


def slot_positions(id_block, capacity, experts):
    rows = id_block.shape[0]
    picks = jnp.concatenate([id_block[:, 0], id_block[:, 1]], axis=0)
    onehot = (picks[:, None] == jnp.arange(experts, dtype=jnp.int32)[None, :]).astype(jnp.int32)
    position = lax.optimization_barrier(jnp.sum((jnp.cumsum(onehot, axis=0) - 1) * onehot, axis=1))
    position = jnp.where(position < capacity, position, -1)
    return jnp.stack([position[:rows], position[rows:]], axis=1).astype(jnp.int32)

def expert_grads(operands):
    expert_in, expert_cot, w_gate, w_up, w_down = operands
    pre_gate = jnp.dot(expert_in, w_gate, preferred_element_type=jnp.float32)
    pre_up = jnp.dot(expert_in, w_up, preferred_element_type=jnp.float32)
    sigmoid_gate = jax.nn.sigmoid(pre_gate)
    active = pre_gate * sigmoid_gate
    hidden = (active * pre_up).astype(jnp.bfloat16)
    grad_down = jnp.dot(hidden.T, expert_cot, preferred_element_type=jnp.float32)
    back_grad = jnp.dot(expert_cot, w_down.T, preferred_element_type=jnp.float32)
    d_gate = (back_grad * pre_up * sigmoid_gate * (1.0 + pre_gate * (1.0 - sigmoid_gate))).astype(jnp.bfloat16)
    d_up = (back_grad * active).astype(jnp.bfloat16)
    grad_gate = jnp.dot(expert_in.T, d_gate, preferred_element_type=jnp.float32)
    grad_up = jnp.dot(expert_in.T, d_up, preferred_element_type=jnp.float32)
    return (grad_gate.astype(jnp.bfloat16), grad_up.astype(jnp.bfloat16), grad_down.astype(jnp.bfloat16))

def reference(context, residual, attn_weight, norm_gain, gate_weight, up_weight, down_weight, cotangent, expert_ids, gate_fixed):
    summed = lax.optimization_barrier(jnp.sum(attn_weight.astype(jnp.float32), axis=0))
    merged = (summed / BRANCHES).astype(jnp.bfloat16)
    feature_block = D // N_MP
    attention = jnp.zeros((TOKENS, D), jnp.float32)
    for block_index in range(N_MP):
        low = block_index * feature_block
        partial_value = jnp.dot(context[:, low:low + feature_block], merged[low:low + feature_block, :], preferred_element_type=jnp.float32)
        partial_value = lax.optimization_barrier(partial_value.astype(jnp.bfloat16))
        attention = attention + partial_value.astype(jnp.float32)
    mixed_in = residual.astype(jnp.float32) + attention
    inv_rms = lax.rsqrt(lax.optimization_barrier(jnp.mean(mixed_in * mixed_in, axis=1, keepdims=True)) + 1e-05)
    normed = (mixed_in * inv_rms * norm_gain.astype(jnp.float32)[None, :]).astype(jnp.bfloat16)
    groups = TOKENS // TOK_DEV
    slots = jax.vmap(lambda blk: slot_positions(blk, CAP, EXPERTS))(expert_ids.reshape(groups, TOK_DEV, 2)).reshape(TOKENS, 2)
    token_index = jnp.arange(TOKENS, dtype=jnp.int32)
    group_index = token_index // TOK_DEV
    is_valid = slots >= 0
    destination = (expert_ids * groups + group_index[:, None]) * CAP + slots
    destination = jnp.where(is_valid, destination, EXPERTS * groups * CAP).astype(jnp.int32)
    slot_token = jnp.full((EXPERTS * groups * CAP,), -1, jnp.int32)
    slot_token = slot_token.at[destination.reshape(-1)].set(jnp.broadcast_to(token_index[:, None], (TOKENS, 2)).reshape(-1), mode='drop')
    slot_gate = jnp.zeros((EXPERTS * groups * CAP,), jnp.float32)
    slot_gate = slot_gate.at[destination.reshape(-1)].set((gate_fixed.astype(jnp.float32) / 32768.0).reshape(-1), mode='drop')
    present = slot_token >= 0
    safe_index = jnp.maximum(slot_token, 0).astype(jnp.int32)
    rows_in = jnp.where(present[:, None], normed[safe_index], jnp.zeros((), jnp.bfloat16))
    rows_cot = (slot_gate[:, None] * cotangent[safe_index].astype(jnp.float32)).astype(jnp.bfloat16)
    rows_in = rows_in.reshape(EXPERTS, groups * CAP, D)
    rows_cot = rows_cot.reshape(EXPERTS, groups * CAP, D)
    results = lax.map(expert_grads, (rows_in, rows_cot, gate_weight, up_weight, down_weight))
    return (results[0], results[1], results[2])
```

```python
import functools

import jax
import jax.numpy as jnp
from jax import lax
from jax.sharding import PartitionSpec as P


def slot_positions(id_block, capacity, experts):
    rows = id_block.shape[0]
    picks = jnp.concatenate([id_block[:, 0], id_block[:, 1]], axis=0)
    onehot = (picks[:, None] == jnp.arange(experts, dtype=jnp.int32)[None, :]).astype(jnp.int32)
    position = jnp.sum((jnp.cumsum(onehot, axis=0) - 1) * onehot, axis=1)
    position = jnp.where(position < capacity, position, -1)
    return jnp.stack([position[:rows], position[rows:]], axis=1)


def shift(value, axis, step):
    size = lax.axis_size(axis)
    return lax.ppermute(value, axis, [(i, (i + step) % size) for i in range(size)])


def flip(value, axis, mask):
    size = lax.axis_size(axis)
    return lax.ppermute(value, axis, [(i, i ^ mask) for i in range(size)])


def after(value, *others):
    return lax.optimization_barrier((value, *others))[0]


def masks(size):
    out, mask = [], size // 2
    while mask >= 1:
        out.append(mask)
        mask //= 2
    return out


def relative_order(size):
    order = [0]
    for mask in masks(size):
        order = order + [o ^ mask for o in order]
    return order


def gather_flips(block, axis, todo):
    for mask in todo:
        block = jnp.concatenate([block, flip(block, axis, mask)], axis=0)
    return block


def line_steps(block, axis):
    size = lax.axis_size(axis)
    up, down, got = block, block, {}
    for k in range(1, size):
        up = got[k] = lax.ppermute(up, axis, [(i, i + 1) for i in range(k - 1, size - 1)])
        down = got[-k] = lax.ppermute(down, axis, [(i + 1, i) for i in range(size - k)])
    return got


def pick_flip(got, axis, mask):
    size, me = lax.axis_size(axis), lax.axis_index(axis)
    value = None
    for k in sorted({i - (i ^ mask) for i in range(size)}, key=abs):
        where = functools.reduce(jnp.logical_or, [me == i for i in range(size) if i - (i ^ mask) == k])
        value = got[k] if value is None else jnp.where(where, got[k], value)
    return value


def plane_gather(block):
    n_mp, n_dp = lax.axis_size("mp"), lax.axis_size("dp")
    half = block.shape[0] // 2
    todo = masks(n_dp)
    across = [block] + [shift(block, "mp", s) for s in range(1, n_mp)]
    if not todo:
        return across
    far = flip(block, "dp", todo[0])
    far_across = [far]
    for s in range(1, n_mp):
        top = shift(far[:half], "mp", s)
        bottom = flip(across[s][half:], "dp", todo[0])
        far_across.append(jnp.concatenate([top, bottom], axis=0))
    across = [jnp.concatenate([a, b], axis=0) for a, b in zip(across, far_across)]
    return [gather_flips(a, "dp", todo[1:]) for a in across]


def whole_columns(across, piece):
    n_mp, n_dp, x = lax.axis_size("mp"), lax.axis_size("dp"), lax.axis_index("mp")
    parts = []
    for p in range(n_mp):
        value = across[0]
        for s in range(1, n_mp):
            value = jnp.where((x - s) % n_mp == p, across[s], value)
        parts.append(value)
    return jnp.concatenate(
        [part[:, k * piece : (k + 1) * piece] for k in range(n_dp) for part in parts], axis=1
    )


def per_device(
    context,
    residual,
    attn_weight,
    norm_gain,
    gate_weight,
    up_weight,
    down_weight,
    cotangent,
    expert_ids,
    gate_fixed,
):
    n_br, n_mp, n_dp = lax.axis_size("branch"), lax.axis_size("mp"), lax.axis_size("dp")
    z, x, d = lax.axis_index("branch"), lax.axis_index("mp"), lax.axis_index("dp")
    tokens, width = residual.shape
    experts = n_br * gate_weight.shape[0]
    capacity = 5 * tokens // (2 * experts)
    piece = width // (n_dp * n_mp)

    def choose(options, index):
        value = options[0]
        for i in range(1, len(options)):
            value = jnp.where(index == i, options[i], value)
        return value

    def cut(value, i):
        return value[:, i * piece : (i + 1) * piece]

    def my_columns(value):
        return jnp.concatenate(
            [choose([cut(value, k * n_mp + p) for p in range(n_mp)], x) for k in range(n_dp)], axis=1
        )

    slots = slot_positions(expert_ids, capacity, experts)
    slot_code = jnp.where(slots >= 0, (expert_ids ^ z) * capacity + slots, -1)
    target = jnp.arange(experts * capacity, dtype=jnp.int32)[:, None]
    matches = [slot_code[:, k][None, :] == target for k in range(2)]
    selector = (matches[0] | matches[1]).astype(jnp.bfloat16)
    gate = gate_fixed.astype(jnp.float32) / 32768.0
    row_gate = sum(jnp.where(matches[k], gate[:, k][None, :], 0.0) for k in range(2))
    row_gate = jnp.sum(row_gate, axis=1, keepdims=True)

    weight = attn_weight[0]
    weight_for = [choose([cut(weight, (p + s) % n_mp) for p in range(n_mp)], x) for s in range(n_mp)]
    steps = line_steps(context, "branch")
    last_steps = (steps[n_br - 1], steps[1 - n_br]) if n_br > 1 else (context,)

    def project(m):
        ctx = context if m == 0 else pick_flip(steps, "branch", m)
        ctx = gather_flips(ctx, "dp", masks(n_dp))
        value = jnp.dot(ctx, weight_for[0], preferred_element_type=jnp.float32)
        for t in range(1, n_mp):
            away = jnp.dot(ctx, weight_for[t], preferred_element_type=jnp.float32).astype(jnp.bfloat16)
            value = value + shift(away, "mp", t).astype(jnp.float32)
        return value

    shares = [project(0)] + [project(m).astype(jnp.bfloat16) for m in range(1, n_br)]

    cot_rows = jnp.dot(selector, my_columns(cotangent), preferred_element_type=jnp.float32)
    send_cot = (cot_rows * row_gate).astype(jnp.bfloat16)
    send_cot = [send_cot[m * capacity : (m + 1) * capacity] for m in range(n_br)]
    send_cot = lax.optimization_barrier((*send_cot, *last_steps))[:n_br]
    cot_slots = [flip(send_cot[m], "branch", m) if m else send_cot[m] for m in range(n_br)]

    back = [flip(shares[m], "branch", m) for m in range(1, n_br)]
    total = shares[0]
    for value in back:
        total = total + value.astype(jnp.float32)
    total = (total / n_br).astype(jnp.bfloat16)

    order = relative_order(n_dp)
    got = [None] * n_dp
    for i, o in enumerate(order):
        block = total[i * tokens : (i + 1) * tokens]
        got[o] = flip(block, "dp", o) if o else block
    attention = jnp.concatenate([choose(got, d ^ k) for k in range(n_dp)], axis=1)
    mixed = my_columns(residual).astype(jnp.float32) + attention.astype(jnp.float32)
    squares = jnp.sum(mixed * mixed, axis=1, keepdims=True)
    all_squares = squares
    for s in range(1, n_mp):
        all_squares = all_squares + shift(squares.reshape(1, tokens), "mp", s).reshape(tokens, 1)
    inv_rms = lax.rsqrt(all_squares / width + 1e-05)
    gain = my_columns(norm_gain[None, :]).astype(jnp.float32)
    normed = (mixed * inv_rms * gain).astype(jnp.bfloat16)
    send_in = jnp.dot(selector, normed, preferred_element_type=jnp.float32).astype(jnp.bfloat16)
    send_in = [send_in[m * capacity : (m + 1) * capacity] for m in range(n_br)]

    near = max(1, n_br // 2)
    bounds = [(lo, hi) for lo, hi in ((0, near), (near, n_br)) if hi > lo]

    def gathered(slots_in):
        return whole_columns(plane_gather(jnp.concatenate(slots_in, axis=0)), piece)

    cot_slots = lax.optimization_barrier((*cot_slots, *shares))[:n_br]
    cotan_rows = jnp.concatenate([gathered(cot_slots[lo:hi]) for lo, hi in bounds], axis=0)
    in_slots = [flip(send_in[m], "branch", m) if m else send_in[m] for m in range(n_br)]
    tokens_in = jnp.concatenate([gathered(in_slots[lo:hi]) for lo, hi in bounds], axis=0)

    w_gate, w_up, w_down = gate_weight[0], up_weight[0], down_weight[0]
    back_grad = lax.dot_general(
        cotan_rows, w_down, (((1,), (1,)), ((), ())), preferred_element_type=jnp.float32
    )
    pre_gate = jnp.dot(tokens_in, w_gate, preferred_element_type=jnp.float32)
    pre_up = jnp.dot(tokens_in, w_up, preferred_element_type=jnp.float32)
    sigmoid_gate = jax.nn.sigmoid(pre_gate)
    active = pre_gate * sigmoid_gate
    hidden = (active * pre_up).astype(jnp.bfloat16)
    d_gate = (back_grad * pre_up * sigmoid_gate * (1.0 + pre_gate * (1.0 - sigmoid_gate))).astype(
        jnp.bfloat16
    )
    d_up = (back_grad * active).astype(jnp.bfloat16)
    contract = (((0,), (0,)), ((), ()))
    grad_gate = lax.dot_general(tokens_in, d_gate, contract, preferred_element_type=jnp.float32)
    grad_up = lax.dot_general(tokens_in, d_up, contract, preferred_element_type=jnp.float32)
    grad_down = lax.dot_general(hidden, cotan_rows, contract, preferred_element_type=jnp.float32)
    return (
        grad_gate.astype(jnp.bfloat16)[None],
        grad_up.astype(jnp.bfloat16)[None],
        grad_down.astype(jnp.bfloat16)[None],
    )


def solution(mesh):
    return jax.shard_map(
        per_device,
        mesh=mesh,
        in_specs=(
            P(("branch", "dp"), "mp"),
            P(("branch", "dp"), None),
            P("branch", "mp", "dp"),
            P(),
            P("branch", None, ("mp", "dp")),
            P("branch", None, ("mp", "dp")),
            P("branch", ("mp", "dp"), None),
            P(("branch", "dp"), None),
            P(("branch", "dp"), None),
            P(("branch", "dp"), None),
        ),
        out_specs=(
            P("branch", None, ("mp", "dp")),
            P("branch", None, ("mp", "dp")),
            P("branch", ("mp", "dp"), None),
        ),
        check_vma=False,
    )
```

```python
import functools

import jax
import jax.numpy as jnp
from jax import lax
from jax.experimental import pallas as pl
from jax.experimental.pallas import tpu as pltpu
from jax.sharding import PartitionSpec as P


def slot_positions(id_block, capacity, experts):
    rows = id_block.shape[0]
    picks = jnp.concatenate([id_block[:, 0], id_block[:, 1]], axis=0)
    onehot = (picks[:, None] == jnp.arange(experts, dtype=jnp.int32)[None, :]).astype(jnp.int32)
    position = jnp.sum((jnp.cumsum(onehot, axis=0) - 1) * onehot, axis=1)
    position = jnp.where(position < capacity, position, -1)
    return jnp.stack([position[:rows], position[rows:]], axis=1)


def shift(value, axis, step):
    size = lax.axis_size(axis)
    return lax.ppermute(value, axis, [(i, (i + step) % size) for i in range(size)])


def flip(value, axis, mask):
    size = lax.axis_size(axis)
    return lax.ppermute(value, axis, [(i, i ^ mask) for i in range(size)])


def masks(size):
    out, mask = [], size // 2
    while mask >= 1:
        out.append(mask)
        mask //= 2
    return out


def relative_order(size):
    order = [0]
    for mask in masks(size):
        order = order + [o ^ mask for o in order]
    return order


def gather_flips(block, axis, todo):
    for mask in todo:
        block = jnp.concatenate([block, flip(block, axis, mask)], axis=0)
    return block


def pick_flip(got, axis, mask):
    size, me = lax.axis_size(axis), lax.axis_index(axis)
    value = None
    for k in sorted({i - (i ^ mask) for i in range(size)}, key=abs):
        where = functools.reduce(jnp.logical_or, [me == i for i in range(size) if i - (i ^ mask) == k])
        value = got[k] if value is None else jnp.where(where, got[k], value)
    return value


def column_kernel(_, value_ref, out_ref):
    out_ref[...] = value_ref[...]


def pick_columns(value, piece, count, stride, first):
    rows = value.shape[0]
    tile = rows if rows <= 512 else 512
    return pl.pallas_call(
        column_kernel,
        grid_spec=pltpu.PrefetchScalarGridSpec(
            num_scalar_prefetch=1,
            grid=(rows // tile, count),
            in_specs=[pl.BlockSpec((tile, piece), lambda i, k, at: (i, k * stride + at[0]))],
            out_specs=pl.BlockSpec((tile, piece), lambda i, k, at: (i, k)),
        ),
        out_shape=jax.ShapeDtypeStruct((rows, count * piece), value.dtype),
    )(jnp.full((1,), first, jnp.int32), value)


def order_kernel(n_mp, n_dp, piece, sources, at, *refs):
    out_ref = refs[-1]
    turn = at[n_mp + pl.program_id(0)]
    for c in range(sources):

        @pl.when(turn == c)
        def _():
            for p in range(n_mp):
                step = at[p]
                for k in range(n_dp):
                    first = (k * n_mp + p) * piece
                    out_ref[:, first : first + piece] = refs[c][step, 0, 0, :, k * piece : (k + 1) * piece]


def order_rows(values, groups, n_dp, piece):
    n_mp, x = values[0].shape[0], lax.axis_index("mp")
    sources, part = len(values), n_dp // len(values)
    slots = sum(len(g) for g in groups)
    rows = values[0].shape[1] // (part * slots)
    places = [(j // part, j % part, m) for g in groups for j in range(n_dp) for m in g]
    count = len(places)
    columns = [[c for c, _, _ in places]]
    for c in range(sources):
        held = next((j, m) for i, j, m in places if i == c)
        kept = []
        for i, j, m in places:
            held = (j, m) if i == c else held
            kept.append(held)
        columns += [[j for j, _ in kept], [m for _, m in kept]]
    steps = (x - jnp.arange(n_mp, dtype=jnp.int32)) % n_mp
    table = jnp.concatenate([steps, jnp.asarray(sum(columns, []), jnp.int32)])

    def spec(c):
        base = n_mp + count * (1 + 2 * c)
        return pl.BlockSpec(
            (n_mp, 1, 1, rows, n_dp * piece), lambda i, at: (0, at[base + i], at[base + count + i], 0, 0)
        )

    return pl.pallas_call(
        functools.partial(order_kernel, n_mp, n_dp, piece, sources),
        grid_spec=pltpu.PrefetchScalarGridSpec(
            num_scalar_prefetch=1,
            grid=(count,),
            in_specs=[spec(c) for c in range(sources)],
            out_specs=pl.BlockSpec((rows, n_mp * n_dp * piece), lambda i, at: (i, 0)),
        ),
        out_shape=jax.ShapeDtypeStruct((count * rows, n_mp * n_dp * piece), values[0].dtype),
        compiler_params=pltpu.CompilerParams(vmem_limit_bytes=32 << 20),
    )(table, *[v.reshape(n_mp, part, slots, rows, n_dp * piece) for v in values])


def whole_columns(across, piece):
    n_mp, n_dp, x = lax.axis_size("mp"), lax.axis_size("dp"), lax.axis_index("mp")
    parts = []
    for p in range(n_mp):
        value = across[0]
        for s in range(1, n_mp):
            value = jnp.where((x - s) % n_mp == p, across[s], value)
        parts.append(value)
    return jnp.concatenate(
        [part[:, k * piece : (k + 1) * piece] for k in range(n_dp) for part in parts], axis=1
    )


def per_device(
    context,
    residual,
    attn_weight,
    norm_gain,
    gate_weight,
    up_weight,
    down_weight,
    cotangent,
    expert_ids,
    gate_fixed,
):
    n_br, n_mp, n_dp = lax.axis_size("branch"), lax.axis_size("mp"), lax.axis_size("dp")
    z, x, d = lax.axis_index("branch"), lax.axis_index("mp"), lax.axis_index("dp")
    tokens, width = residual.shape
    experts = n_br * gate_weight.shape[0]
    capacity = 5 * tokens // (2 * experts)
    piece = width // (n_dp * n_mp)
    hidden_width = gate_weight.shape[2]
    padded_width = -(-hidden_width // 128) * 128

    def choose(options, index):
        value = options[0]
        for i in range(1, len(options)):
            value = jnp.where(index == i, options[i], value)
        return value

    def my_columns(value):
        return pick_columns(value, piece, n_dp, n_mp, x)

    def choose(options, index):
        value = options[0]
        for i in range(1, len(options)):
            value = jnp.where(index == i, options[i], value)
        return value

    far_masks = masks(n_dp)[:1]
    core_masks = masks(n_dp)[1:]
    near = n_br // 2
    groups = [g for g in ([0], list(range(1, near + 1)), list(range(near + 1, n_br))) if g]

    live = {}

    def fence():
        names = sorted(live)
        for name, value in zip(names, lax.optimization_barrier(tuple(live[n] for n in names))):
            live[name] = value

    def hop_plane(name, g):
        for m in groups[g]:
            if m:
                live[f"{name}{m}"] = flip(live[f"{name}{m}"], "branch", m)

    def hop_near(name, g):
        block = jnp.concatenate([live.pop(f"{name}{m}") for m in groups[g]], axis=0)
        live[f"{name}a{g}_0"] = block
        for s in range(1, n_mp):
            live[f"{name}a{g}_{s}"] = shift(block, "mp", s)
        for mask in far_masks:
            live[f"{name}f{g}"] = flip(block, "dp", mask)

    def hop_far(name, g):
        across = [live.pop(f"{name}a{g}_{t}") for t in range(n_mp)]
        parts = [across[0]]
        if far_masks:
            far = live.pop(f"{name}f{g}")
            half = far.shape[0] // 2
            parts += [far]
            for t in range(1, n_mp):
                parts += [across[t], shift(far[:half], "mp", t), flip(across[t][half:], "dp", far_masks[0])]
        else:
            parts += across[1:]
        live[f"{name}a{g}"] = jnp.concatenate(parts, axis=0)

    def hop_rest(name, g):
        block = live[f"{name}a{g}"]
        block = block.reshape(n_mp, -1, block.shape[1])
        for mask in core_masks:
            block = jnp.concatenate([block, flip(block, "dp", mask)], axis=1)
        live[f"{name}a{g}"] = block

    def finish(name, g):
        block = live.pop(f"{name}a{g}")
        return whole_columns([block[t] for t in range(n_mp)], piece)

    def cascade(name, at):
        for g in range(len(groups)):
            for lag, hop in ((0, hop_plane), (1, hop_near), (2, hop_far), (3, hop_rest)):
                if at == g - 1 + lag:
                    hop(name, g)

    slots = slot_positions(expert_ids, capacity, experts)
    slot_code = jnp.where(slots >= 0, (expert_ids ^ z) * capacity + slots, -1)
    target = jnp.arange(experts * capacity, dtype=jnp.int32)[:, None]
    matches = [slot_code[:, k][None, :] == target for k in range(2)]
    selector = (matches[0] | matches[1]).astype(jnp.bfloat16)
    gate = gate_fixed.astype(jnp.float32) / 32768.0
    row_gate = sum(jnp.where(matches[k], gate[:, k][None, :], 0.0) for k in range(2))
    row_gate = jnp.sum(row_gate, axis=1, keepdims=True)

    live["weight"] = attn_weight[0]
    live["selector"], live["row_gate"] = selector, row_gate
    live["up0"], live["down0"], live["ctx0"] = context, context, context
    live["cotangent"], live["residual"], live["gain"] = cotangent, residual, norm_gain[None, :]

    def distance(m):
        return max(abs(i - (i ^ m)) for i in range(n_br))

    for r in range(n_br + 3):
        if r + 1 < n_br:
            k = r + 1
            live[f"up{k}"] = lax.ppermute(live[f"up{r}"], "branch", [(i, i + 1) for i in range(r, n_br - 1)])
            live[f"down{k}"] = lax.ppermute(live[f"down{r}"], "branch", [(i + 1, i) for i in range(n_br - k)])
        for m in range(n_br):
            s = distance(m)
            if r == s and m:
                got = {k: live[f"up{k}" if k > 0 else f"down{-k}"] for k in {i - (i ^ m) for i in range(n_br)}}
                live[f"ctx{m}"] = pick_flip(got, "branch", m)
            if r == s:
                live[f"ctx{m}"] = gather_flips(live[f"ctx{m}"], "dp", far_masks)
            if r == s + 1:
                live[f"ctx{m}"] = gather_flips(live[f"ctx{m}"], "dp", core_masks)
            if r == s + 2:
                ctx = live.pop(f"ctx{m}")
                for t in list(range(1, n_mp)) + [0]:
                    product = jnp.dot(ctx, live[f"weight{t}"], preferred_element_type=jnp.float32)
                    product = product.astype(jnp.bfloat16)
                    live[f"part{m}_{t}"] = shift(product, "mp", t) if t else product
            if r == s + 3 or (r == n_br + 2 and s + 3 > r):
                share = sum(live.pop(f"part{m}_{t}").astype(jnp.float32) for t in range(n_mp))
                live[f"share{m}"] = flip(share.astype(jnp.bfloat16), "branch", m) if m else share
        if r == 1:
            weight = live.pop("weight")
            cut = [weight[:, p * piece : (p + 1) * piece] for p in range(n_mp)]
            for t in range(n_mp):
                live[f"weight{t}"] = choose([cut[(p + t) % n_mp] for p in range(n_mp)], x)
        if r == 2:
            rows = jnp.dot(live["selector"], my_columns(live.pop("cotangent")), preferred_element_type=jnp.float32)
            rows = (rows * live.pop("row_gate")).astype(jnp.bfloat16)
            for m in range(n_br):
                live[f"cot{m}"] = rows[m * capacity : (m + 1) * capacity]
        if r == n_br + 2:
            pad = jnp.zeros((width, padded_width - hidden_width), gate_weight.dtype)
            live["gate_up"] = jnp.concatenate([gate_weight[0], pad, up_weight[0]], axis=1)
        if r == n_br:
            live["residual"] = my_columns(live["residual"])
            live["gain"] = my_columns(live["gain"])
        if n_br - 1 <= r < n_br + 1 and r - n_br + 2 < len(groups):
            hop_plane("cot", r - n_br + 2)
        if r == n_br:
            block = live["cot_first"] = jnp.concatenate([live.pop(f"cot{m}") for m in range(near + 1)], axis=0)
            live["cot_first_far"] = flip(block, "dp", far_masks[0])
        if r == n_br + 1:
            block = jnp.concatenate([live.pop(f"cot{m}") for m in range(near + 1, n_br)], axis=0)
            far = jnp.concatenate([live.pop("cot_first_far"), flip(block, "dp", far_masks[0])], axis=0)
            block = jnp.concatenate([live.pop("cot_first"), block], axis=0)
            live["cot"], live["cot_far"] = block, far
            for t in range(1, n_mp):
                live[f"cot_top{t}"] = shift(block[: near * capacity], "mp", t)
        if r == n_br + 2:
            block, far = live.pop("cot"), live.pop("cot_far")
            parts = [block, far]
            first = (near + 1) * capacity
            both = jnp.concatenate([block[near * capacity :], far[near * capacity : first]], axis=0)
            rest = block.shape[0] - near * capacity
            for t in range(1, n_mp):
                top = live.pop(f"cot_top{t}")
                across = shift(both, "mp", t)
                parts += [top, across[:rest], flip(top, "dp", far_masks[0]), across[rest:]]
                live[f"cot_end{t}"] = far[first:]
            live["cota0"] = jnp.concatenate(parts[:2], axis=0)
            live["cota_across"] = jnp.concatenate(parts[2:], axis=0)
        fence()

    total = sum(live.pop(f"share{m}").astype(jnp.float32) for m in range(n_br))
    total = (total / n_br).astype(jnp.bfloat16)
    got = [None] * n_dp
    for i, o in enumerate(relative_order(n_dp)):
        block = total[i * tokens : (i + 1) * tokens]
        got[o] = flip(block, "dp", o) if o else block
    parts, across = [live.pop("cota0")], live.pop("cota_across")
    size = across.shape[0] // (n_mp - 1) if n_mp > 1 else 0
    for t in range(1, n_mp):
        parts += [across[(t - 1) * size : t * size], shift(live.pop(f"cot_end{t}"), "mp", t)]
    for i, part in enumerate(parts):
        live[f"cot_part{i}"] = part
    cot_parts = len(parts)
    live["attention"] = jnp.concatenate([choose(got, d ^ k) for k in range(n_dp)], axis=1)
    fence()

    mixed = live.pop("residual").astype(jnp.float32) + live.pop("attention").astype(jnp.float32)
    squares = jnp.sum(mixed * mixed, axis=1, keepdims=True)
    all_squares = squares
    for s in range(1, n_mp):
        all_squares = all_squares + shift(squares.reshape(1, tokens), "mp", s).reshape(tokens, 1)
    live["mixed"], live["squares"] = mixed, all_squares
    fence()

    inv_rms = lax.rsqrt(live.pop("squares") / width + 1e-05)
    normed = (live.pop("mixed") * inv_rms * live.pop("gain").astype(jnp.float32)).astype(jnp.bfloat16)
    send_in = jnp.dot(live.pop("selector"), normed, preferred_element_type=jnp.float32).astype(jnp.bfloat16)
    for m in range(n_br):
        live[f"in{m}"] = send_in[m * capacity : (m + 1) * capacity]
    for r in range(len(groups) + 2):
        cascade("in", r)
        if r == 0:
            live["cota0"] = jnp.concatenate([live.pop(f"cot_part{i}") for i in range(cot_parts)], axis=0)
            for c in range(1, 1 << len(core_masks)):
                live[f"cota{c}"] = flip(live["cota0"], "dp", sum(v for i, v in enumerate(core_masks) if c >> i & 1))
        if r == 1:
            blocks = [live.pop(f"cota{c}") for c in range(1 << len(core_masks))]
            live["cotan"] = order_rows([v.reshape(n_mp, -1, n_dp * piece) for v in blocks], groups, n_dp, piece)
        if r == 2:
            live["back"] = lax.dot_general(
                live["cotan"], down_weight[0], (((1,), (1,)), ((), ())), preferred_element_type=jnp.float32
            )
        fence()
    cotan_rows, back_grad = live.pop("cotan"), live.pop("back")
    tokens_in = jnp.concatenate([finish("in", g) for g in range(len(groups))], axis=0)
    pre = jnp.dot(tokens_in, live.pop("gate_up"), preferred_element_type=jnp.float32)
    pre_gate, pre_up = pre[:, :hidden_width], pre[:, padded_width:]
    sigmoid_gate = jax.nn.sigmoid(pre_gate)
    active = pre_gate * sigmoid_gate
    hidden = (active * pre_up).astype(jnp.bfloat16)
    d_gate = (back_grad * pre_up * sigmoid_gate * (1.0 + pre_gate * (1.0 - sigmoid_gate))).astype(jnp.bfloat16)
    d_up = (back_grad * active).astype(jnp.bfloat16)
    contract = (((0,), (0,)), ((), ()))
    grads = []
    for left, right in ((tokens_in, d_gate), (tokens_in, d_up), (hidden, cotan_rows)):
        grad = lax.dot_general(left, right, contract, preferred_element_type=jnp.float32)
        grads.append(grad.astype(jnp.bfloat16)[None])
    return tuple(grads)


def solution(mesh):
    return jax.shard_map(
        per_device,
        mesh=mesh,
        in_specs=(
            P(("branch", "dp"), "mp"),
            P(("branch", "dp"), None),
            P("branch", "mp", "dp"),
            P(),
            P("branch", None, ("mp", "dp")),
            P("branch", None, ("mp", "dp")),
            P("branch", ("mp", "dp"), None),
            P(("branch", "dp"), None),
            P(("branch", "dp"), None),
            P(("branch", "dp"), None),
        ),
        out_specs=(
            P("branch", None, ("mp", "dp")),
            P("branch", None, ("mp", "dp")),
            P("branch", ("mp", "dp"), None),
        ),
        check_vma=False,
    )
```

```python
import functools

import jax
import jax.numpy as jnp
from jax import lax
from jax.experimental import pallas as pl
from jax.experimental.pallas import tpu as pltpu
from jax.sharding import PartitionSpec as P


def slot_positions(id_block, capacity, experts):
    rows = id_block.shape[0]
    picks = jnp.concatenate([id_block[:, 0], id_block[:, 1]], axis=0)
    onehot = (picks[:, None] == jnp.arange(experts, dtype=jnp.int32)[None, :]).astype(jnp.int32)
    position = jnp.sum((jnp.cumsum(onehot, axis=0) - 1) * onehot, axis=1)
    position = jnp.where(position < capacity, position, -1)
    return jnp.stack([position[:rows], position[rows:]], axis=1)


def shift(value, axis, step):
    size = lax.axis_size(axis)
    return lax.ppermute(value, axis, [(i, (i + step) % size) for i in range(size)])


def flip(value, axis, mask):
    size = lax.axis_size(axis)
    return lax.ppermute(value, axis, [(i, i ^ mask) for i in range(size)])


def masks(size):
    out, mask = [], size // 2
    while mask >= 1:
        out.append(mask)
        mask //= 2
    return out


def relative_order(size):
    order = [0]
    for mask in masks(size):
        order = order + [o ^ mask for o in order]
    return order


def gather_flips(block, axis, todo):
    for mask in todo:
        block = jnp.concatenate([block, flip(block, axis, mask)], axis=0)
    return block


def pick_flip(got, axis, mask):
    size, me = lax.axis_size(axis), lax.axis_index(axis)
    value = None
    for k in sorted({i - (i ^ mask) for i in range(size)}, key=abs):
        where = functools.reduce(jnp.logical_or, [me == i for i in range(size) if i - (i ^ mask) == k])
        value = got[k] if value is None else jnp.where(where, got[k], value)
    return value


def column_kernel(_, value_ref, out_ref):
    out_ref[...] = value_ref[...]


def pick_columns(value, piece, count, stride, first):
    rows = value.shape[0]
    tile = rows if rows <= 512 else 512
    return pl.pallas_call(
        column_kernel,
        grid_spec=pltpu.PrefetchScalarGridSpec(
            num_scalar_prefetch=1,
            grid=(rows // tile, count),
            in_specs=[pl.BlockSpec((tile, piece), lambda i, k, at: (i, k * stride + at[0]))],
            out_specs=pl.BlockSpec((tile, piece), lambda i, k, at: (i, k)),
        ),
        out_shape=jax.ShapeDtypeStruct((rows, count * piece), value.dtype),
    )(jnp.full((1,), first, jnp.int32), value)


def order_kernel(n_mp, n_dp, piece, sources, at, *refs):
    out_ref = refs[-1]
    turn = at[n_mp + pl.program_id(0)]
    for c in range(sources):

        @pl.when(turn == c)
        def _():
            for p in range(n_mp):
                step = at[p]
                for k in range(n_dp):
                    first = (k * n_mp + p) * piece
                    out_ref[:, first : first + piece] = refs[c][step, 0, 0, :, k * piece : (k + 1) * piece]


def order_rows(sources, groups, n_dp, piece):
    values, where = [], {}
    for slots, parts in sources:
        share = n_dp // len(parts)
        for c, value in enumerate(parts):
            for j in range(share):
                for i, m in enumerate(slots):
                    where[c * share + j, m] = (len(values), j, i)
            n_mp, columns = value.shape[0], value.shape[2]
            values.append(value.reshape(n_mp, share, len(slots), -1, columns))
    rows = values[0].shape[3]
    x = lax.axis_index("mp")
    places = [where[j, m] for g in groups for j in range(n_dp) for m in g]
    count = len(places)
    columns = [[c for c, _, _ in places]]
    for c in range(len(values)):
        held = next((j, m) for i, j, m in places if i == c)
        kept = []
        for i, j, m in places:
            held = (j, m) if i == c else held
            kept.append(held)
        columns += [[j for j, _ in kept], [m for _, m in kept]]
    steps = (x - jnp.arange(n_mp, dtype=jnp.int32)) % n_mp
    table = jnp.concatenate([steps, jnp.asarray(sum(columns, []), jnp.int32)])

    def spec(c):
        base = n_mp + count * (1 + 2 * c)
        return pl.BlockSpec(
            (n_mp, 1, 1, rows, n_dp * piece), lambda i, at: (0, at[base + i], at[base + count + i], 0, 0)
        )

    return pl.pallas_call(
        functools.partial(order_kernel, n_mp, n_dp, piece, len(values)),
        grid_spec=pltpu.PrefetchScalarGridSpec(
            num_scalar_prefetch=1,
            grid=(count,),
            in_specs=[spec(c) for c in range(len(values))],
            out_specs=pl.BlockSpec((rows, n_mp * n_dp * piece), lambda i, at: (i, 0)),
        ),
        out_shape=jax.ShapeDtypeStruct((count * rows, n_mp * n_dp * piece), values[0].dtype),
        compiler_params=pltpu.CompilerParams(vmem_limit_bytes=40 << 20),
    )(table, *values)


def forward_kernel(rows_ref, gate_ref, up_ref, back_ref, hidden_ref, d_gate_ref, d_up_ref):
    contract = (((1,), (1,)), ((), ()))
    rows = rows_ref[...]
    pre_gate = lax.dot_general(gate_ref[...], rows, contract, preferred_element_type=jnp.float32)
    pre_up = lax.dot_general(up_ref[...], rows, contract, preferred_element_type=jnp.float32)
    back = back_ref[...]
    sigmoid_gate = jax.nn.sigmoid(pre_gate)
    active = pre_gate * sigmoid_gate
    hidden_ref[...] = (active * pre_up).astype(jnp.bfloat16)
    d_gate = back * pre_up * sigmoid_gate * (1.0 + pre_gate * (1.0 - sigmoid_gate))
    d_gate_ref[...] = d_gate.astype(jnp.bfloat16)
    d_up_ref[...] = (back * active).astype(jnp.bfloat16)


def fitting(size, most):
    return next((t for t in range(most, 127, -128) if size % t == 0), size)


def forward(rows, gate_t, up_t, back):
    count, width = rows.shape
    units = gate_t.shape[0]
    tile = fitting(count, 256)
    weights = pl.BlockSpec((units, width), lambda i: (0, 0))
    part = pl.BlockSpec((units, tile), lambda i: (0, i))
    return pl.pallas_call(
        forward_kernel,
        grid=(count // tile,),
        in_specs=[pl.BlockSpec((tile, width), lambda i: (i, 0)), weights, weights, part],
        out_specs=[part] * 3,
        out_shape=[jax.ShapeDtypeStruct((units, count), jnp.bfloat16)] * 3,
        compiler_params=pltpu.CompilerParams(vmem_limit_bytes=56 << 20),
    )(rows, gate_t, up_t, back)


def gradient_kernel(rows_ref, cot_ref, hidden_ref, d_gate_ref, d_up_ref, gate_ref, up_ref, down_ref):
    rows = rows_ref[...]
    pairs = ((d_gate_ref[...], rows, gate_ref), (d_up_ref[...], rows, up_ref), (hidden_ref[...], cot_ref[...], down_ref))
    for left, right, out_ref in pairs:
        out_ref[...] = jnp.dot(left, right, preferred_element_type=jnp.float32).astype(jnp.bfloat16)


def gradients(rows, cot, hidden, d_gate, d_up):
    count, width = rows.shape
    units = hidden.shape[0]
    tile = fitting(width, 512)
    columns = pl.BlockSpec((count, tile), lambda i: (0, i))
    held = pl.BlockSpec((units, count), lambda i: (0, 0))
    return pl.pallas_call(
        gradient_kernel,
        grid=(width // tile,),
        in_specs=[columns, columns, held, held, held],
        out_specs=[pl.BlockSpec((units, tile), lambda i: (0, i))] * 3,
        out_shape=[jax.ShapeDtypeStruct((units, width), jnp.bfloat16)] * 3,
        compiler_params=pltpu.CompilerParams(vmem_limit_bytes=56 << 20),
    )(rows, cot, hidden, d_gate, d_up)


def per_device(
    context,
    residual,
    attn_weight,
    norm_gain,
    gate_weight,
    up_weight,
    down_weight,
    cotangent,
    expert_ids,
    gate_fixed,
):
    n_br, n_mp, n_dp = lax.axis_size("branch"), lax.axis_size("mp"), lax.axis_size("dp")
    z, x, d = lax.axis_index("branch"), lax.axis_index("mp"), lax.axis_index("dp")
    tokens, width = residual.shape
    experts = n_br * gate_weight.shape[0]
    capacity = 5 * tokens // (2 * experts)
    piece = width // (n_dp * n_mp)

    def choose(options, index):
        value = options[0]
        for i in range(1, len(options)):
            value = jnp.where(index == i, options[i], value)
        return value

    def my_columns(value):
        return pick_columns(value, piece, n_dp, n_mp, x)

    def choose(options, index):
        value = options[0]
        for i in range(1, len(options)):
            value = jnp.where(index == i, options[i], value)
        return value

    far_masks = masks(n_dp)[:1]
    core_masks = masks(n_dp)[1:]
    near = n_br // 2
    groups = [g for g in ([0], list(range(1, near + 1)), list(range(near + 1, n_br))) if g]

    live = {}

    def fence():
        names = sorted(live)
        for name, value in zip(names, lax.optimization_barrier(tuple(live[n] for n in names))):
            live[name] = value

    def hop_plane(name, g):
        for m in groups[g]:
            if m:
                live[f"{name}{m}"] = flip(live[f"{name}{m}"], "branch", m)

    def hop_near(name, g):
        block = jnp.concatenate([live.pop(f"{name}{m}") for m in groups[g]], axis=0)
        live[f"{name}a{g}_0"] = block
        for s in range(1, n_mp):
            live[f"{name}a{g}_{s}"] = shift(block, "mp", s)
        for mask in far_masks:
            live[f"{name}f{g}"] = flip(block, "dp", mask)

    def hop_far(name, g):
        across = [live.pop(f"{name}a{g}_{t}") for t in range(n_mp)]
        parts = [across[0]]
        if far_masks:
            far = live.pop(f"{name}f{g}")
            half = far.shape[0] // 2
            parts += [far]
            for t in range(1, n_mp):
                parts += [across[t], shift(far[:half], "mp", t), flip(across[t][half:], "dp", far_masks[0])]
        else:
            parts += across[1:]
        live[f"{name}a{g}"] = jnp.concatenate(parts, axis=0)

    def core_flips(block):
        flips = [sum(v for i, v in enumerate(core_masks) if c >> i & 1) for c in range(1 << len(core_masks))]
        return [flip(block, "dp", mask) if mask else block for mask in flips]

    def hop_rest(name, g):
        for c, block in enumerate(core_flips(live.pop(f"{name}a{g}"))):
            live[f"{name}a{g}_{c}"] = block

    def taken(name):
        blocks = [live.pop(f"{name}_{c}") for c in range(1 << len(core_masks))]
        return [v.reshape(n_mp, -1, v.shape[1]) for v in blocks]

    def cascade(name, at):
        for g in range(len(groups)):
            for lag, hop in ((0, hop_plane), (1, hop_near), (2, hop_far), (3, hop_rest)):
                if at == g - 1 + lag:
                    hop(name, g)

    slots = slot_positions(expert_ids, capacity, experts)
    slot_code = jnp.where(slots >= 0, (expert_ids ^ z) * capacity + slots, -1)
    target = jnp.arange(experts * capacity, dtype=jnp.int32)[:, None]
    matches = [slot_code[:, k][None, :] == target for k in range(2)]
    selector = (matches[0] | matches[1]).astype(jnp.bfloat16)
    gate = gate_fixed.astype(jnp.float32) / 32768.0
    row_gate = sum(jnp.where(matches[k], gate[:, k][None, :], 0.0) for k in range(2))
    row_gate = jnp.sum(row_gate, axis=1, keepdims=True)

    live["weight"] = attn_weight[0]
    live["selector"], live["row_gate"] = selector, row_gate
    live["up0"], live["down0"], live["ctx0"] = context, context, context
    live["cotangent"], live["residual"], live["gain"] = cotangent, residual, norm_gain[None, :]

    def distance(m):
        return max(abs(i - (i ^ m)) for i in range(n_br))

    for r in range(n_br + 3):
        if r + 1 < n_br:
            k = r + 1
            live[f"up{k}"] = lax.ppermute(live[f"up{r}"], "branch", [(i, i + 1) for i in range(r, n_br - 1)])
            live[f"down{k}"] = lax.ppermute(live[f"down{r}"], "branch", [(i + 1, i) for i in range(n_br - k)])
        for m in range(n_br):
            s = distance(m)
            if r == s and m:
                got = {k: live[f"up{k}" if k > 0 else f"down{-k}"] for k in {i - (i ^ m) for i in range(n_br)}}
                live[f"ctx{m}"] = pick_flip(got, "branch", m)
            if r == s:
                live[f"ctx{m}"] = gather_flips(live[f"ctx{m}"], "dp", far_masks)
            if r == s + 1:
                live[f"ctx{m}"] = gather_flips(live[f"ctx{m}"], "dp", core_masks)
            if r == s + 2:
                ctx = live.pop(f"ctx{m}")
                for t in list(range(1, n_mp)) + [0]:
                    product = jnp.dot(ctx, live[f"weight{t}"], preferred_element_type=jnp.float32)
                    product = product.astype(jnp.bfloat16)
                    live[f"part{m}_{t}"] = shift(product, "mp", t) if t else product
            if r == s + 3 or (r == n_br + 2 and s + 3 > r):
                share = sum(live.pop(f"part{m}_{t}").astype(jnp.float32) for t in range(n_mp))
                live[f"share{m}"] = flip(share.astype(jnp.bfloat16), "branch", m) if m else share
        if r == 1:
            weight = live.pop("weight")
            cut = [weight[:, p * piece : (p + 1) * piece] for p in range(n_mp)]
            for t in range(n_mp):
                live[f"weight{t}"] = choose([cut[(p + t) % n_mp] for p in range(n_mp)], x)
        if r == 2:
            rows = jnp.dot(live["selector"], my_columns(live.pop("cotangent")), preferred_element_type=jnp.float32)
            rows = (rows * live.pop("row_gate")).astype(jnp.bfloat16)
            for m in range(n_br):
                live[f"cot{m}"] = rows[m * capacity : (m + 1) * capacity]
        if r == n_br:
            live["residual"] = my_columns(live["residual"])
            live["gain"] = my_columns(live["gain"])
        if n_br - 1 <= r < n_br + 1 and r - n_br + 2 < len(groups):
            hop_plane("cot", r - n_br + 2)
        if r == n_br:
            block = live["cot_first"] = jnp.concatenate([live.pop(f"cot{m}") for m in range(near + 1)], axis=0)
            live["cot_first_far"] = flip(block, "dp", far_masks[0])
        if r == n_br + 1:
            block = jnp.concatenate([live.pop(f"cot{m}") for m in range(near + 1, n_br)], axis=0)
            far = jnp.concatenate([live.pop("cot_first_far"), flip(block, "dp", far_masks[0])], axis=0)
            block = jnp.concatenate([live.pop("cot_first"), block], axis=0)
            live["cot"], live["cot_far"] = block, far
            for t in range(1, n_mp):
                live[f"cot_top{t}"] = shift(block[: near * capacity], "mp", t)
        if r == n_br + 2:
            block, far = live.pop("cot"), live.pop("cot_far")
            parts = [block, far]
            first = (near + 1) * capacity
            both = jnp.concatenate([block[near * capacity :], far[near * capacity : first]], axis=0)
            rest = block.shape[0] - near * capacity
            for t in range(1, n_mp):
                top = live.pop(f"cot_top{t}")
                across = shift(both, "mp", t)
                parts += [top, across[:rest], flip(top, "dp", far_masks[0]), across[rest:]]
                live[f"cot_end{t}"] = far[first:]
            live["cota0"] = jnp.concatenate(parts[:2], axis=0)
            live["cota_across"] = jnp.concatenate(parts[2:], axis=0)
        fence()

    total = sum(live.pop(f"share{m}").astype(jnp.float32) for m in range(n_br))
    total = (total / n_br).astype(jnp.bfloat16)
    got = [None] * n_dp
    for i, o in enumerate(relative_order(n_dp)):
        block = total[i * tokens : (i + 1) * tokens]
        got[o] = flip(block, "dp", o) if o else block
    parts, across = [live.pop("cota0")], live.pop("cota_across")
    size = across.shape[0] // (n_mp - 1) if n_mp > 1 else 0
    for t in range(1, n_mp):
        parts += [across[(t - 1) * size : t * size], shift(live.pop(f"cot_end{t}"), "mp", t)]
    for i, part in enumerate(parts):
        live[f"cot_part{i}"] = part
    cot_parts = len(parts)
    live["attention"] = jnp.concatenate([choose(got, d ^ k) for k in range(n_dp)], axis=1)
    fence()

    mixed = live.pop("residual").astype(jnp.float32) + live.pop("attention").astype(jnp.float32)
    squares = jnp.sum(mixed * mixed, axis=1, keepdims=True)
    all_squares = squares
    for s in range(1, n_mp):
        all_squares = all_squares + shift(squares.reshape(1, tokens), "mp", s).reshape(tokens, 1)
    live["mixed"], live["squares"] = mixed, all_squares
    fence()

    inv_rms = lax.rsqrt(live.pop("squares") / width + 1e-05)
    normed = (live.pop("mixed") * inv_rms * live.pop("gain").astype(jnp.float32)).astype(jnp.bfloat16)
    send_in = jnp.dot(live.pop("selector"), normed, preferred_element_type=jnp.float32).astype(jnp.bfloat16)
    for m in range(n_br):
        live[f"in{m}"] = send_in[m * capacity : (m + 1) * capacity]
    for r in range(len(groups) + 2):
        cascade("in", r)
        if r == 0:
            live["cota0"] = jnp.concatenate([live.pop(f"cot_part{i}") for i in range(cot_parts)], axis=0)
            for c, block in enumerate(core_flips(live.pop("cota0"))):
                live[f"cota_{c}"] = block
        if r == 1:
            live["cotan"] = order_rows([(list(range(n_br)), taken("cota"))], groups, n_dp, piece)
        if r == 2:
            live["back"] = lax.dot_general(
                down_weight[0], live["cotan"], (((1,), (1,)), ((), ())), preferred_element_type=jnp.float32
            )
        fence()
    cotan_rows, back_grad = live.pop("cotan"), live.pop("back")
    sources = [(slots_of, taken(f"ina{g}")) for g, slots_of in enumerate(groups)]
    tokens_in = order_rows(sources, groups, n_dp, piece)
    hidden, d_gate, d_up = forward(tokens_in, gate_weight[0].T, up_weight[0].T, back_grad)
    grad_gate, grad_up, grad_down = gradients(tokens_in, cotan_rows, hidden, d_gate, d_up)
    return (grad_gate.T[None], grad_up.T[None], grad_down[None])


def solution(mesh):
    return jax.shard_map(
        per_device,
        mesh=mesh,
        in_specs=(
            P(("branch", "dp"), "mp"),
            P(("branch", "dp"), None),
            P("branch", "mp", "dp"),
            P(),
            P("branch", None, ("mp", "dp")),
            P("branch", None, ("mp", "dp")),
            P("branch", ("mp", "dp"), None),
            P(("branch", "dp"), None),
            P(("branch", "dp"), None),
            P(("branch", "dp"), None),
        ),
        out_specs=(
            P("branch", None, ("mp", "dp")),
            P("branch", None, ("mp", "dp")),
            P("branch", ("mp", "dp"), None),
        ),
        check_vma=False,
    )
```

```python
import functools

import jax
import jax.numpy as jnp
from jax import lax
from jax.experimental import pallas as pl
from jax.experimental.pallas import tpu as pltpu
from jax.sharding import PartitionSpec as P


def slot_positions(id_block, capacity, experts):
    rows = id_block.shape[0]
    picks = jnp.concatenate([id_block[:, 0], id_block[:, 1]], axis=0)
    onehot = (picks[:, None] == jnp.arange(experts, dtype=jnp.int32)[None, :]).astype(jnp.int32)
    position = jnp.sum((jnp.cumsum(onehot, axis=0) - 1) * onehot, axis=1)
    position = jnp.where(position < capacity, position, -1)
    return jnp.stack([position[:rows], position[rows:]], axis=1)


def shift(value, axis, step):
    size = lax.axis_size(axis)
    return lax.ppermute(value, axis, [(i, (i + step) % size) for i in range(size)])


def flip(value, axis, mask):
    size = lax.axis_size(axis)
    return lax.ppermute(value, axis, [(i, i ^ mask) for i in range(size)])


def masks(size):
    out, mask = [], size // 2
    while mask >= 1:
        out.append(mask)
        mask //= 2
    return out


def relative_order(size):
    order = [0]
    for mask in masks(size):
        order = order + [o ^ mask for o in order]
    return order


def gather_flips(block, axis, todo):
    for mask in todo:
        block = jnp.concatenate([block, flip(block, axis, mask)], axis=0)
    return block


def pick_flip(got, axis, mask):
    size, me = lax.axis_size(axis), lax.axis_index(axis)
    value = None
    for k in sorted({i - (i ^ mask) for i in range(size)}, key=abs):
        where = functools.reduce(jnp.logical_or, [me == i for i in range(size) if i - (i ^ mask) == k])
        value = got[k] if value is None else jnp.where(where, got[k], value)
    return value


def column_kernel(_, value_ref, out_ref):
    out_ref[...] = value_ref[...]


def pick_columns(value, piece, count, stride, first):
    rows = value.shape[0]
    tile = rows if rows <= 512 else 512
    return pl.pallas_call(
        column_kernel,
        grid_spec=pltpu.PrefetchScalarGridSpec(
            num_scalar_prefetch=1,
            grid=(rows // tile, count),
            in_specs=[pl.BlockSpec((tile, piece), lambda i, k, at: (i, k * stride + at[0]))],
            out_specs=pl.BlockSpec((tile, piece), lambda i, k, at: (i, k)),
        ),
        out_shape=jax.ShapeDtypeStruct((rows, count * piece), value.dtype),
    )(jnp.full((1,), first, jnp.int32), value)


def order_kernel(n_mp, n_dp, piece, steps, at, *refs):
    out_ref = refs[-1]
    count = pl.num_programs(0)
    for p in range(n_mp):
        for c, step in enumerate(steps):

            @pl.when((at[p] == step) & (at[n_mp + step * count + pl.program_id(0)] == c))
            def _():
                for k in range(n_dp):
                    first = (k * n_mp + p) * piece
                    out_ref[:, first : first + piece] = refs[c][0, :, k * piece : (k + 1) * piece]


def order_rows(sources, groups, n_dp, piece, first=0, total=None, whole=None):
    rows = sources[0][1].shape[1]
    n_mp, x = lax.axis_size("mp"), lax.axis_index("mp")
    places = [(j, m) for g in groups for j in range(n_dp) for m in g]
    count = len(places)
    steps = [step for step, _, _ in sources]
    columns = []
    for step in range(n_mp):
        mine = [c for c, other in enumerate(steps) if other == step]
        columns += [next(c for c in mine if place in sources[c][2]) for place in places]
    for _, _, blocks in sources:
        held = next(blocks[place] for place in places if place in blocks)
        for place in places:
            held = blocks.get(place, held)
            columns.append(held)
    table = jnp.concatenate([(x - jnp.arange(n_mp, dtype=jnp.int32)) % n_mp, jnp.asarray(columns, jnp.int32)])

    def spec(c):
        base = n_mp + count * (n_mp + c)
        return pl.BlockSpec((1, rows, n_dp * piece), lambda i, at: (at[base + i], 0, 0))

    more = [] if whole is None else [whole]
    return pl.pallas_call(
        functools.partial(order_kernel, n_mp, n_dp, piece, steps),
        grid_spec=pltpu.PrefetchScalarGridSpec(
            num_scalar_prefetch=1,
            grid=(count,),
            in_specs=[spec(c) for c in range(len(sources))] + [pl.BlockSpec(memory_space=pltpu.HBM)] * len(more),
            out_specs=pl.BlockSpec((rows, n_mp * n_dp * piece), lambda i, at: (first + i, 0)),
        ),
        out_shape=pltpu.HBM(((total or count) * rows, n_mp * n_dp * piece), sources[0][1].dtype),
        input_output_aliases={1 + len(sources): 0} if more else {},
        compiler_params=pltpu.CompilerParams(vmem_limit_bytes=40 << 20),
    )(table, *[value for _, value, _ in sources], *more)


def forward_kernel(rows_ref, gate_ref, up_ref, back_ref, hidden_ref, d_gate_ref, d_up_ref):
    contract = (((1,), (1,)), ((), ()))
    rows = rows_ref[...]
    pre_gate = lax.dot_general(gate_ref[...], rows, contract, preferred_element_type=jnp.float32)
    pre_up = lax.dot_general(up_ref[...], rows, contract, preferred_element_type=jnp.float32)
    back = back_ref[...]
    sigmoid_gate = jax.nn.sigmoid(pre_gate)
    active = pre_gate * sigmoid_gate
    hidden_ref[...] = (active * pre_up).astype(jnp.bfloat16)
    d_gate = back * pre_up * sigmoid_gate * (1.0 + pre_gate * (1.0 - sigmoid_gate))
    d_gate_ref[...] = d_gate.astype(jnp.bfloat16)
    d_up_ref[...] = (back * active).astype(jnp.bfloat16)


def fitting(size, most):
    return next((t for t in range(most, 127, -128) if size % t == 0), size)


def forward(rows, gate_t, up_t, back):
    count, width = rows.shape
    units = gate_t.shape[0]
    tile = fitting(count, 256)
    weights = pl.BlockSpec((units, width), lambda i: (0, 0))
    part = pl.BlockSpec((units, tile), lambda i: (0, i))
    return pl.pallas_call(
        forward_kernel,
        grid=(count // tile,),
        in_specs=[pl.BlockSpec((tile, width), lambda i: (i, 0)), weights, weights, part],
        out_specs=[part] * 3,
        out_shape=[jax.ShapeDtypeStruct((units, count), jnp.bfloat16)] * 3,
        compiler_params=pltpu.CompilerParams(vmem_limit_bytes=56 << 20),
    )(rows, gate_t, up_t, back)


def gradient_kernel(rows_ref, cot_ref, hidden_ref, d_gate_ref, d_up_ref, gate_ref, up_ref, down_ref):
    rows = rows_ref[...]
    pairs = ((d_gate_ref[...], rows, gate_ref), (d_up_ref[...], rows, up_ref), (hidden_ref[...], cot_ref[...], down_ref))
    for left, right, out_ref in pairs:
        out_ref[...] = jnp.dot(left, right, preferred_element_type=jnp.float32).astype(jnp.bfloat16)


def gradients(rows, cot, hidden, d_gate, d_up):
    count, width = rows.shape
    units = hidden.shape[0]
    tile = fitting(width, 512)
    columns = pl.BlockSpec((count, tile), lambda i: (0, i))
    held = pl.BlockSpec((units, count), lambda i: (0, 0))
    return pl.pallas_call(
        gradient_kernel,
        grid=(width // tile,),
        in_specs=[columns, columns, held, held, held],
        out_specs=[pl.BlockSpec((units, tile), lambda i: (0, i))] * 3,
        out_shape=[jax.ShapeDtypeStruct((units, width), jnp.bfloat16)] * 3,
        compiler_params=pltpu.CompilerParams(vmem_limit_bytes=56 << 20),
    )(rows, cot, hidden, d_gate, d_up)


def per_device(
    context,
    residual,
    attn_weight,
    norm_gain,
    gate_weight,
    up_weight,
    down_weight,
    cotangent,
    expert_ids,
    gate_fixed,
):
    n_br, n_mp, n_dp = lax.axis_size("branch"), lax.axis_size("mp"), lax.axis_size("dp")
    z, x, d = lax.axis_index("branch"), lax.axis_index("mp"), lax.axis_index("dp")
    tokens, width = residual.shape
    experts = n_br * gate_weight.shape[0]
    capacity = 5 * tokens // (2 * experts)
    piece = width // (n_dp * n_mp)

    def choose(options, index):
        value = options[0]
        for i in range(1, len(options)):
            value = jnp.where(index == i, options[i], value)
        return value

    def my_columns(value):
        return pick_columns(value, piece, n_dp, n_mp, x)

    def choose(options, index):
        value = options[0]
        for i in range(1, len(options)):
            value = jnp.where(index == i, options[i], value)
        return value

    far_masks = masks(n_dp)[:1]
    core_masks = masks(n_dp)[1:]
    near = n_br // 2
    groups = [g for g in ([0], list(range(1, near + 1)), list(range(near + 1, n_br))) if g]

    live = {}

    def fence():
        names = sorted(live)
        for name, value in zip(names, lax.optimization_barrier(tuple(live[n] for n in names))):
            live[name] = value

    def hop_plane(name, g):
        for m in groups[g]:
            if m:
                live[f"{name}{m}"] = flip(live[f"{name}{m}"], "branch", m)

    def hop_near(name, g):
        block = jnp.concatenate([live.pop(f"{name}{m}") for m in groups[g]], axis=0)
        live[f"{name}a{g}_0"] = block
        for s in range(1, n_mp):
            live[f"{name}a{g}_{s}"] = shift(block, "mp", s)
        for mask in far_masks:
            live[f"{name}f{g}"] = flip(block, "dp", mask)

    def hop_far(name, g):
        across = [live.pop(f"{name}a{g}_{t}") for t in range(n_mp)]
        parts = [across[0]]
        if far_masks:
            far = live.pop(f"{name}f{g}")
            half = far.shape[0] // 2
            parts += [far]
            for t in range(1, n_mp):
                parts += [across[t], shift(far[:half], "mp", t), flip(across[t][half:], "dp", far_masks[0])]
        else:
            parts += across[1:]
        live[f"{name}a{g}"] = jnp.concatenate(parts, axis=0)

    def core_flips(block):
        flips = [sum(v for i, v in enumerate(core_masks) if c >> i & 1) for c in range(1 << len(core_masks))]
        return [flip(block, "dp", mask) if mask else block for mask in flips]

    def hop_rest(name, g):
        for c, block in enumerate(core_flips(live.pop(f"{name}a{g}"))):
            live[f"{name}a{g}_{c}"] = block

    def taken(name):
        blocks = [live.pop(f"{name}_{c}") for c in range(1 << len(core_masks))]
        return [v.reshape(-1, capacity, v.shape[1]) for v in blocks]

    def cascade(name, at):
        for g in range(len(groups)):
            for lag, hop in ((0, hop_plane), (1, hop_near), (2, hop_far), (3, hop_rest)):
                if at == g - 1 + lag:
                    hop(name, g)

    slots = slot_positions(expert_ids, capacity, experts)
    slot_code = jnp.where(slots >= 0, (expert_ids ^ z) * capacity + slots, -1)
    target = jnp.arange(experts * capacity, dtype=jnp.int32)[:, None]
    matches = [slot_code[:, k][None, :] == target for k in range(2)]
    selector = (matches[0] | matches[1]).astype(jnp.bfloat16)
    gate = gate_fixed.astype(jnp.float32) / 32768.0
    row_gate = sum(jnp.where(matches[k], gate[:, k][None, :], 0.0) for k in range(2))
    row_gate = jnp.sum(row_gate, axis=1, keepdims=True)

    live["weight"] = attn_weight[0]
    live["selector"], live["row_gate"] = selector, row_gate
    live["up0"], live["down0"], live["ctx0"] = context, context, context
    live["cotangent"], live["residual"], live["gain"] = cotangent, residual, norm_gain[None, :]

    def distance(m):
        return max(abs(i - (i ^ m)) for i in range(n_br))

    for r in range(n_br + 3):
        if r + 1 < n_br:
            k = r + 1
            live[f"up{k}"] = lax.ppermute(live[f"up{r}"], "branch", [(i, i + 1) for i in range(r, n_br - 1)])
            live[f"down{k}"] = lax.ppermute(live[f"down{r}"], "branch", [(i + 1, i) for i in range(n_br - k)])
        for m in range(n_br):
            s = distance(m)
            if r == s and m:
                got = {k: live[f"up{k}" if k > 0 else f"down{-k}"] for k in {i - (i ^ m) for i in range(n_br)}}
                live[f"ctx{m}"] = pick_flip(got, "branch", m)
            if r == s:
                live[f"ctx{m}"] = gather_flips(live[f"ctx{m}"], "dp", far_masks)
            if r == s + 1:
                live[f"ctx{m}"] = gather_flips(live[f"ctx{m}"], "dp", core_masks)
            if r == s + 2:
                ctx = live.pop(f"ctx{m}")
                for t in list(range(1, n_mp)) + [0]:
                    product = jnp.dot(ctx, live[f"weight{t}"], preferred_element_type=jnp.float32)
                    product = product.astype(jnp.bfloat16)
                    live[f"part{m}_{t}"] = shift(product, "mp", t) if t else product
            if r == s + 3 or (r == n_br + 2 and s + 3 > r):
                share = sum(live.pop(f"part{m}_{t}").astype(jnp.float32) for t in range(n_mp))
                live[f"share{m}"] = flip(share.astype(jnp.bfloat16), "branch", m) if m else share
        if r == 1:
            weight = live.pop("weight")
            cut = [weight[:, p * piece : (p + 1) * piece] for p in range(n_mp)]
            for t in range(n_mp):
                live[f"weight{t}"] = choose([cut[(p + t) % n_mp] for p in range(n_mp)], x)
        if r == 2:
            rows = jnp.dot(live["selector"], my_columns(live.pop("cotangent")), preferred_element_type=jnp.float32)
            rows = (rows * live.pop("row_gate")).astype(jnp.bfloat16)
            for m in range(n_br):
                live[f"cot{m}"] = rows[m * capacity : (m + 1) * capacity]
        if r == n_br + 2:
            live["residual"] = my_columns(live["residual"])
            live["gain"] = my_columns(live["gain"])
        if n_br - 1 <= r < n_br + 1 and r - n_br + 2 < len(groups):
            hop_plane("cot", r - n_br + 2)
        if r == n_br:
            block = live["cot_near"] = jnp.concatenate([live.pop(f"cot{m}") for m in range(near)], axis=0)
            live["cot_near_far"] = flip(block, "dp", far_masks[0])
        if r == n_br + 1:
            block = live["cot_rest"] = jnp.concatenate([live.pop(f"cot{m}") for m in range(near, n_br)], axis=0)
            live["cot_rest_far"] = flip(block, "dp", far_masks[0])
            for t in range(1, n_mp):
                live[f"cot_near_{t}"] = shift(live["cot_near"], "mp", t)
        if r == n_br + 2:
            both = jnp.concatenate([live["cot_rest"], live["cot_rest_far"][:capacity]], axis=0)
            for t in range(1, n_mp):
                live[f"cot_both_{t}"] = shift(both, "mp", t)
                live[f"cot_near_far_{t}"] = flip(live[f"cot_near_{t}"], "dp", far_masks[0])
        fence()

    total = sum(live.pop(f"share{m}").astype(jnp.float32) for m in range(n_br))
    total = (total / n_br).astype(jnp.bfloat16)
    got = [None] * n_dp
    for i, o in enumerate(relative_order(n_dp)):
        block = total[i * tokens : (i + 1) * tokens]
        got[o] = flip(block, "dp", o) if o else block
    split = n_br - near > 1
    if split:
        for t in range(1, n_mp):
            live[f"cot_end_{t}"] = shift(live["cot_rest_far"][capacity:], "mp", t)
    parts = [live[f"cot_{name}"] for name in ("near", "rest", "near_far", "rest_far")]
    rest = parts[1].shape[0]
    for t in range(1, n_mp):
        both = live.pop(f"cot_both_{t}")
        parts += [live.pop(f"cot_near_{t}"), both[:rest], live.pop(f"cot_near_far_{t}"), both[rest:]]
    live["cota"] = jnp.concatenate(parts, axis=0)
    for name in ("near", "rest", "near_far", "rest_far"):
        del live[f"cot_{name}"]
    live["attention"] = jnp.concatenate([choose(got, d ^ k) for k in range(n_dp)], axis=1)
    fence()

    mixed = live.pop("residual").astype(jnp.float32) + live.pop("attention").astype(jnp.float32)
    squares = jnp.sum(mixed * mixed, axis=1, keepdims=True)
    all_squares = squares
    for s in range(1, n_mp):
        all_squares = all_squares + shift(squares.reshape(1, tokens), "mp", s).reshape(tokens, 1)
    live["mixed"], live["squares"] = mixed, all_squares
    if split:
        ends = jnp.concatenate([live.pop(f"cot_end_{t}") for t in range(1, n_mp)], axis=0)
        for c, block in enumerate(core_flips(ends)):
            live[f"cotend_{c}"] = block
    fence()

    inv_rms = lax.rsqrt(live.pop("squares") / width + 1e-05)
    normed = (live.pop("mixed") * inv_rms * live.pop("gain").astype(jnp.float32)).astype(jnp.bfloat16)
    send_in = jnp.dot(live.pop("selector"), normed, preferred_element_type=jnp.float32).astype(jnp.bfloat16)
    for m in range(n_br):
        live[f"in{m}"] = send_in[m * capacity : (m + 1) * capacity]

    def order_group(g):
        first = n_dp * sum(len(other) for other in groups[:g])
        slots_of, share = groups[g], 1 + len(far_masks)
        sources = []
        for c, value in enumerate(taken(f"ina{g}")):
            for t in range(n_mp):
                at = {
                    (c * share + y, m): (t * share + y) * len(slots_of) + i
                    for y in range(share)
                    for i, m in enumerate(slots_of)
                }
                sources.append((t, value, at))
        live["in"] = order_rows(sources, [slots_of], n_dp, piece, first, n_dp * n_br, live.get("in"))

    for r in range(len(groups) + 2):
        if 0 <= r - 3 < len(groups):
            order_group(r - 3)
        cascade("in", r)
        if r == 0:
            for c, block in enumerate(core_flips(live.pop("cota"))):
                live[f"cota_{c}"] = block
        if r == 1:
            sources = []
            for c, value in enumerate(taken("cota")):
                for t in range(n_mp):
                    base = t * (n_br + near + 1) + (n_br - near - 1 if t else 0)
                    at = {(2 * c, m): base + m for m in range(n_br)}
                    at.update({(2 * c + 1, m): base + n_br + m for m in range(near + 1 if t else n_br)})
                    sources.append((t, value, at))
            for c, value in enumerate(taken("cotend") if split else []):
                for t in range(1, n_mp):
                    base = (t - 1) * (n_br - near - 1) - near - 1
                    sources.append((t, value, {(2 * c + 1, m): base + m for m in range(near + 1, n_br)}))
            live["cotan"] = order_rows(sources, groups, n_dp, piece)
        if r == 2:
            live["back"] = lax.dot_general(
                down_weight[0], live["cotan"], (((1,), (1,)), ((), ())), preferred_element_type=jnp.float32
            )
        fence()
    cotan_rows, back_grad = live.pop("cotan"), live.pop("back")
    order_group(len(groups) - 1)
    tokens_in = live.pop("in")
    hidden, d_gate, d_up = forward(tokens_in, gate_weight[0].T, up_weight[0].T, back_grad)
    grad_gate, grad_up, grad_down = gradients(tokens_in, cotan_rows, hidden, d_gate, d_up)
    return (grad_gate.T[None], grad_up.T[None], grad_down[None])


def solution(mesh):
    return jax.shard_map(
        per_device,
        mesh=mesh,
        in_specs=(
            P(("branch", "dp"), "mp"),
            P(("branch", "dp"), None),
            P("branch", "mp", "dp"),
            P(),
            P("branch", None, ("mp", "dp")),
            P("branch", None, ("mp", "dp")),
            P("branch", ("mp", "dp"), None),
            P(("branch", "dp"), None),
            P(("branch", "dp"), None),
            P(("branch", "dp"), None),
        ),
        out_specs=(
            P("branch", None, ("mp", "dp")),
            P("branch", None, ("mp", "dp")),
            P("branch", ("mp", "dp"), None),
        ),
        check_vma=False,
    )
```

```python
import functools

import jax
import jax.numpy as jnp
from jax import lax
from jax.experimental import pallas as pl
from jax.experimental.pallas import tpu as pltpu
from jax.sharding import PartitionSpec as P


def slot_positions(id_block, capacity, experts):
    rows = id_block.shape[0]
    picks = jnp.concatenate([id_block[:, 0], id_block[:, 1]], axis=0)
    onehot = (picks[:, None] == jnp.arange(experts, dtype=jnp.int32)[None, :]).astype(jnp.int32)
    position = jnp.sum((jnp.cumsum(onehot, axis=0) - 1) * onehot, axis=1)
    position = jnp.where(position < capacity, position, -1)
    return jnp.stack([position[:rows], position[rows:]], axis=1)


def shift(value, axis, step):
    size = lax.axis_size(axis)
    return lax.ppermute(value, axis, [(i, (i + step) % size) for i in range(size)])


def flip(value, axis, mask):
    size = lax.axis_size(axis)
    return lax.ppermute(value, axis, [(i, i ^ mask) for i in range(size)])


def masks(size):
    out, mask = [], size // 2
    while mask >= 1:
        out.append(mask)
        mask //= 2
    return out


def relative_order(size):
    order = [0]
    for mask in masks(size):
        order = order + [o ^ mask for o in order]
    return order


def gather_flips(block, axis, todo):
    for mask in todo:
        block = jnp.concatenate([block, flip(block, axis, mask)], axis=0)
    return block


def pick_flip(got, axis, mask):
    size, me = lax.axis_size(axis), lax.axis_index(axis)
    value = None
    for k in sorted({i - (i ^ mask) for i in range(size)}, key=abs):
        where = functools.reduce(jnp.logical_or, [me == i for i in range(size) if i - (i ^ mask) == k])
        value = got[k] if value is None else jnp.where(where, got[k], value)
    return value


def column_kernel(_, value_ref, out_ref):
    out_ref[...] = value_ref[...]


def pick_columns(value, piece, count, stride, first):
    rows = value.shape[0]
    tile = rows if rows <= 512 else 512
    return pl.pallas_call(
        column_kernel,
        grid_spec=pltpu.PrefetchScalarGridSpec(
            num_scalar_prefetch=1,
            grid=(rows // tile, count),
            in_specs=[pl.BlockSpec((tile, piece), lambda i, k, at: (i, k * stride + at[0]))],
            out_specs=pl.BlockSpec((tile, piece), lambda i, k, at: (i, k)),
        ),
        out_shape=jax.ShapeDtypeStruct((rows, count * piece), value.dtype),
    )(jnp.full((1,), first, jnp.int32), value)


def order_kernel(n_mp, n_dp, piece, steps, at, *refs):
    out_ref = refs[-1]
    count = pl.num_programs(0)
    for p in range(n_mp):
        for c, step in enumerate(steps):

            @pl.when((at[p] == step) & (at[n_mp + step * count + pl.program_id(0)] == c))
            def _():
                for k in range(n_dp):
                    first = (k * n_mp + p) * piece
                    out_ref[:, first : first + piece] = refs[c][0, :, k * piece : (k + 1) * piece]


def order_rows(sources, groups, n_dp, piece, first=0, total=None, whole=None):
    rows = sources[0][1].shape[1]
    n_mp, x = lax.axis_size("mp"), lax.axis_index("mp")
    places = [(j, m) for g in groups for j in range(n_dp) for m in g]
    count = len(places)
    steps = [step for step, _, _ in sources]
    columns = []
    for step in range(n_mp):
        mine = [c for c, other in enumerate(steps) if other == step]
        columns += [next(c for c in mine if place in sources[c][2]) for place in places]
    for _, _, blocks in sources:
        held = next(blocks[place] for place in places if place in blocks)
        for place in places:
            held = blocks.get(place, held)
            columns.append(held)
    table = jnp.concatenate([(x - jnp.arange(n_mp, dtype=jnp.int32)) % n_mp, jnp.asarray(columns, jnp.int32)])

    def spec(c):
        base = n_mp + count * (n_mp + c)
        return pl.BlockSpec((1, rows, n_dp * piece), lambda i, at: (at[base + i], 0, 0))

    more = [] if whole is None else [whole]
    return pl.pallas_call(
        functools.partial(order_kernel, n_mp, n_dp, piece, steps),
        grid_spec=pltpu.PrefetchScalarGridSpec(
            num_scalar_prefetch=1,
            grid=(count,),
            in_specs=[spec(c) for c in range(len(sources))] + [pl.BlockSpec(memory_space=pltpu.HBM)] * len(more),
            out_specs=pl.BlockSpec((rows, n_mp * n_dp * piece), lambda i, at: (first + i, 0)),
        ),
        out_shape=pltpu.HBM(((total or count) * rows, n_mp * n_dp * piece), sources[0][1].dtype),
        input_output_aliases={1 + len(sources): 0} if more else {},
        compiler_params=pltpu.CompilerParams(vmem_limit_bytes=40 << 20),
    )(table, *[value for _, value, _ in sources], *more)


def forward_kernel(rows_ref, gate_ref, up_ref, back_ref, *refs):
    hidden_ref, d_gate_ref, d_up_ref = refs[-3:]
    contract = (((1,), (1,)), ((), ()))
    rows = rows_ref[...]
    pre_gate = lax.dot_general(gate_ref[...], rows, contract, preferred_element_type=jnp.float32)
    pre_up = lax.dot_general(up_ref[...], rows, contract, preferred_element_type=jnp.float32)
    back = back_ref[...]
    sigmoid_gate = jax.nn.sigmoid(pre_gate)
    active = pre_gate * sigmoid_gate
    hidden_ref[...] = (active * pre_up).astype(jnp.bfloat16)
    d_gate = back * pre_up * sigmoid_gate * (1.0 + pre_gate * (1.0 - sigmoid_gate))
    d_gate_ref[...] = d_gate.astype(jnp.bfloat16)
    d_up_ref[...] = (back * active).astype(jnp.bfloat16)


def fitting(size, most):
    return next((t for t in range(most, 127, -128) if size % t == 0), size)


def forward(rows, gate_t, up_t, back, first, last, before=()):
    count, width = rows.shape
    units = gate_t.shape[0]
    tile = fitting(count, 256)
    weights = pl.BlockSpec((units, width), lambda i: (0, 0))
    part = pl.BlockSpec((units, tile), lambda i: (0, first + i))
    return pl.pallas_call(
        forward_kernel,
        grid=(last - first,),
        in_specs=[pl.BlockSpec((tile, width), lambda i: (first + i, 0)), weights, weights, part]
        + [pl.BlockSpec(memory_space=pltpu.HBM)] * len(before),
        out_specs=[part] * 3,
        out_shape=[pltpu.HBM((units, count), jnp.bfloat16)] * 3,
        input_output_aliases={4 + i: i for i in range(len(before))},
        compiler_params=pltpu.CompilerParams(vmem_limit_bytes=56 << 20),
    )(rows, gate_t, up_t, back, *before)


def gradient_kernel(rows_ref, cot_ref, hidden_ref, d_gate_ref, d_up_ref, gate_ref, up_ref, down_ref):
    rows = rows_ref[...]
    pairs = ((d_gate_ref[...], rows, gate_ref), (d_up_ref[...], rows, up_ref), (hidden_ref[...], cot_ref[...], down_ref))
    for left, right, out_ref in pairs:
        out_ref[...] = jnp.dot(left, right, preferred_element_type=jnp.float32).astype(jnp.bfloat16)


def gradients(rows, cot, hidden, d_gate, d_up):
    count, width = rows.shape
    units = hidden.shape[0]
    tile = fitting(width, 512)
    columns = pl.BlockSpec((count, tile), lambda i: (0, i))
    held = pl.BlockSpec((units, count), lambda i: (0, 0))
    return pl.pallas_call(
        gradient_kernel,
        grid=(width // tile,),
        in_specs=[columns, columns, held, held, held],
        out_specs=[pl.BlockSpec((units, tile), lambda i: (0, i))] * 3,
        out_shape=[jax.ShapeDtypeStruct((units, width), jnp.bfloat16)] * 3,
        compiler_params=pltpu.CompilerParams(vmem_limit_bytes=56 << 20),
    )(rows, cot, hidden, d_gate, d_up)


def per_device(
    context,
    residual,
    attn_weight,
    norm_gain,
    gate_weight,
    up_weight,
    down_weight,
    cotangent,
    expert_ids,
    gate_fixed,
):
    n_br, n_mp, n_dp = lax.axis_size("branch"), lax.axis_size("mp"), lax.axis_size("dp")
    z, x, d = lax.axis_index("branch"), lax.axis_index("mp"), lax.axis_index("dp")
    tokens, width = residual.shape
    experts = n_br * gate_weight.shape[0]
    capacity = 5 * tokens // (2 * experts)
    piece = width // (n_dp * n_mp)

    def choose(options, index):
        value = options[0]
        for i in range(1, len(options)):
            value = jnp.where(index == i, options[i], value)
        return value

    def my_columns(value):
        return pick_columns(value, piece, n_dp, n_mp, x)

    def choose(options, index):
        value = options[0]
        for i in range(1, len(options)):
            value = jnp.where(index == i, options[i], value)
        return value

    far_masks = masks(n_dp)[:1]
    core_masks = masks(n_dp)[1:]
    near = n_br // 2
    groups = [g for g in ([0], list(range(1, near + 1)), list(range(near + 1, n_br))) if g]

    live = {}

    def fence():
        names = sorted(live)
        for name, value in zip(names, lax.optimization_barrier(tuple(live[n] for n in names))):
            live[name] = value

    def hop_plane(name, g):
        for m in groups[g]:
            if m:
                live[f"{name}{m}"] = flip(live[f"{name}{m}"], "branch", m)

    def hop_near(name, g):
        block = jnp.concatenate([live.pop(f"{name}{m}") for m in groups[g]], axis=0)
        live[f"{name}a{g}_0"] = block
        for s in range(1, n_mp):
            live[f"{name}a{g}_{s}"] = shift(block, "mp", s)
        for mask in far_masks:
            live[f"{name}f{g}"] = flip(block, "dp", mask)

    def hop_far(name, g):
        across = [live.pop(f"{name}a{g}_{t}") for t in range(n_mp)]
        parts = [across[0]]
        if far_masks:
            far = live.pop(f"{name}f{g}")
            half = far.shape[0] // 2
            parts += [far]
            for t in range(1, n_mp):
                parts += [across[t], shift(far[:half], "mp", t), flip(across[t][half:], "dp", far_masks[0])]
        else:
            parts += across[1:]
        live[f"{name}a{g}"] = jnp.concatenate(parts, axis=0)

    def core_flips(block):
        flips = [sum(v for i, v in enumerate(core_masks) if c >> i & 1) for c in range(1 << len(core_masks))]
        return [flip(block, "dp", mask) if mask else block for mask in flips]

    def hop_rest(name, g):
        for c, block in enumerate(core_flips(live.pop(f"{name}a{g}"))):
            live[f"{name}a{g}_{c}"] = block

    def taken(name):
        blocks = [live.pop(f"{name}_{c}") for c in range(1 << len(core_masks))]
        return [v.reshape(-1, capacity, v.shape[1]) for v in blocks]

    def cascade(name, at):
        for g in range(len(groups)):
            for lag, hop in ((0, hop_plane), (1, hop_near), (2, hop_far), (3, hop_rest)):
                if at == g - 1 + lag:
                    hop(name, g)

    slots = slot_positions(expert_ids, capacity, experts)
    slot_code = jnp.where(slots >= 0, (expert_ids ^ z) * capacity + slots, -1)
    target = jnp.arange(experts * capacity, dtype=jnp.int32)[:, None]
    matches = [slot_code[:, k][None, :] == target for k in range(2)]
    selector = (matches[0] | matches[1]).astype(jnp.bfloat16)
    gate = gate_fixed.astype(jnp.float32) / 32768.0
    row_gate = sum(jnp.where(matches[k], gate[:, k][None, :], 0.0) for k in range(2))
    row_gate = jnp.sum(row_gate, axis=1, keepdims=True)

    live["weight"] = attn_weight[0]
    live["selector"], live["row_gate"] = selector, row_gate
    live["up0"], live["down0"], live["ctx0"] = context, context, context
    live["cotangent"], live["residual"], live["gain"] = cotangent, residual, norm_gain[None, :]

    def distance(m):
        return max(abs(i - (i ^ m)) for i in range(n_br))

    for r in range(n_br + 3):
        if r + 1 < n_br:
            k = r + 1
            live[f"up{k}"] = lax.ppermute(live[f"up{r}"], "branch", [(i, i + 1) for i in range(r, n_br - 1)])
            live[f"down{k}"] = lax.ppermute(live[f"down{r}"], "branch", [(i + 1, i) for i in range(n_br - k)])
        for m in range(n_br):
            s = distance(m)
            if r == s and m:
                got = {k: live[f"up{k}" if k > 0 else f"down{-k}"] for k in {i - (i ^ m) for i in range(n_br)}}
                live[f"ctx{m}"] = pick_flip(got, "branch", m)
            if r == s:
                live[f"ctx{m}"] = gather_flips(live[f"ctx{m}"], "dp", far_masks)
            if r == s + 1:
                live[f"ctx{m}"] = gather_flips(live[f"ctx{m}"], "dp", core_masks)
            if r == s + 2:
                ctx = live.pop(f"ctx{m}")
                for t in list(range(1, n_mp)) + [0]:
                    product = jnp.dot(ctx, live[f"weight{t}"], preferred_element_type=jnp.float32)
                    product = product.astype(jnp.bfloat16)
                    live[f"part{m}_{t}"] = shift(product, "mp", t) if t else product
            if r == s + 3 or (r == n_br + 2 and s + 3 > r):
                share = sum(live.pop(f"part{m}_{t}").astype(jnp.float32) for t in range(n_mp))
                live[f"share{m}"] = flip(share.astype(jnp.bfloat16), "branch", m) if m else share
        if r == 1:
            weight = live.pop("weight")
            cut = [weight[:, p * piece : (p + 1) * piece] for p in range(n_mp)]
            for t in range(n_mp):
                live[f"weight{t}"] = choose([cut[(p + t) % n_mp] for p in range(n_mp)], x)
        if r == 2:
            rows = jnp.dot(live["selector"], my_columns(live.pop("cotangent")), preferred_element_type=jnp.float32)
            rows = (rows * live.pop("row_gate")).astype(jnp.bfloat16)
            for m in range(n_br):
                live[f"cot{m}"] = rows[m * capacity : (m + 1) * capacity]
        if r == n_br + 2:
            live["residual"] = my_columns(live["residual"])
            live["gain"] = my_columns(live["gain"])
        if n_br - 1 <= r < n_br + 1 and r - n_br + 2 < len(groups):
            hop_plane("cot", r - n_br + 2)
        if r == n_br:
            block = live["cot_near"] = jnp.concatenate([live.pop(f"cot{m}") for m in range(near)], axis=0)
            live["cot_near_far"] = flip(block, "dp", far_masks[0])
        if r == n_br + 1:
            block = live["cot_rest"] = jnp.concatenate([live.pop(f"cot{m}") for m in range(near, n_br)], axis=0)
            live["cot_rest_far"] = flip(block, "dp", far_masks[0])
            for t in range(1, n_mp):
                live[f"cot_near_{t}"] = shift(live["cot_near"], "mp", t)
        if r == n_br + 2:
            both = jnp.concatenate([live["cot_rest"], live["cot_rest_far"][:capacity]], axis=0)
            for t in range(1, n_mp):
                live[f"cot_both_{t}"] = shift(both, "mp", t)
                live[f"cot_near_far_{t}"] = flip(live[f"cot_near_{t}"], "dp", far_masks[0])
        fence()

    total = sum(live.pop(f"share{m}").astype(jnp.float32) for m in range(n_br))
    total = (total / n_br).astype(jnp.bfloat16)
    got = [None] * n_dp
    for i, o in enumerate(relative_order(n_dp)):
        block = total[i * tokens : (i + 1) * tokens]
        got[o] = flip(block, "dp", o) if o else block
    split = n_br - near > 1
    if split:
        for t in range(1, n_mp):
            live[f"cot_end_{t}"] = shift(live["cot_rest_far"][capacity:], "mp", t)
    parts = [live[f"cot_{name}"] for name in ("near", "rest", "near_far", "rest_far")]
    rest = parts[1].shape[0]
    for t in range(1, n_mp):
        both = live.pop(f"cot_both_{t}")
        parts += [live.pop(f"cot_near_{t}"), both[:rest], live.pop(f"cot_near_far_{t}"), both[rest:]]
    live["cota"] = jnp.concatenate(parts, axis=0)
    for name in ("near", "rest", "near_far", "rest_far"):
        del live[f"cot_{name}"]
    live["attention"] = jnp.concatenate([choose(got, d ^ k) for k in range(n_dp)], axis=1)
    fence()

    mixed = live.pop("residual").astype(jnp.float32) + live.pop("attention").astype(jnp.float32)
    squares = jnp.sum(mixed * mixed, axis=1, keepdims=True)
    all_squares = squares
    for s in range(1, n_mp):
        all_squares = all_squares + shift(squares.reshape(1, tokens), "mp", s).reshape(tokens, 1)
    live["mixed"], live["squares"] = mixed, all_squares
    if split:
        ends = jnp.concatenate([live.pop(f"cot_end_{t}") for t in range(1, n_mp)], axis=0)
        for c, block in enumerate(core_flips(ends)):
            live[f"cotend_{c}"] = block
    fence()

    inv_rms = lax.rsqrt(live.pop("squares") / width + 1e-05)
    normed = (live.pop("mixed") * inv_rms * live.pop("gain").astype(jnp.float32)).astype(jnp.bfloat16)
    send_in = jnp.dot(live.pop("selector"), normed, preferred_element_type=jnp.float32).astype(jnp.bfloat16)
    for m in range(n_br):
        live[f"in{m}"] = send_in[m * capacity : (m + 1) * capacity]

    def order_group(g):
        first = n_dp * sum(len(other) for other in groups[:g])
        slots_of, share = groups[g], 1 + len(far_masks)
        sources = []
        for c, value in enumerate(taken(f"ina{g}")):
            for t in range(n_mp):
                at = {
                    (c * share + y, m): (t * share + y) * len(slots_of) + i
                    for y in range(share)
                    for i, m in enumerate(slots_of)
                }
                sources.append((t, value, at))
        live["in"] = order_rows(sources, [slots_of], n_dp, piece, first, n_dp * n_br, live.get("in"))

    tile = fitting(n_dp * n_br * capacity, 256)
    early = n_dp * capacity // tile
    for r in range(len(groups) + 2):
        if 0 <= r - 3 < len(groups):
            order_group(r - 3)
        if r == 3 and early:
            live["made0"], live["made1"], live["made2"] = forward(
                live["in"], gate_weight[0].T, up_weight[0].T, live["back"], 0, early
            )
        cascade("in", r)
        if r == 0:
            for c, block in enumerate(core_flips(live.pop("cota"))):
                live[f"cota_{c}"] = block
        if r == 1:
            sources = []
            for c, value in enumerate(taken("cota")):
                for t in range(n_mp):
                    base = t * (n_br + near + 1) + (n_br - near - 1 if t else 0)
                    at = {(2 * c, m): base + m for m in range(n_br)}
                    at.update({(2 * c + 1, m): base + n_br + m for m in range(near + 1 if t else n_br)})
                    sources.append((t, value, at))
            for c, value in enumerate(taken("cotend") if split else []):
                for t in range(1, n_mp):
                    base = (t - 1) * (n_br - near - 1) - near - 1
                    sources.append((t, value, {(2 * c + 1, m): base + m for m in range(near + 1, n_br)}))
            live["cotan"] = order_rows(sources, groups, n_dp, piece)
        if r == 2:
            live["back"] = lax.dot_general(
                down_weight[0], live["cotan"], (((1,), (1,)), ((), ())), preferred_element_type=jnp.float32
            )
        fence()
    cotan_rows, back_grad = live.pop("cotan"), live.pop("back")
    order_group(len(groups) - 1)
    tokens_in = live.pop("in")
    hidden, d_gate, d_up = forward(
        tokens_in, gate_weight[0].T, up_weight[0].T, back_grad, early, tokens_in.shape[0] // tile,
        [live.pop(f"made{i}") for i in range(3)] if early else [],
    )
    grad_gate, grad_up, grad_down = gradients(tokens_in, cotan_rows, hidden, d_gate, d_up)
    return (grad_gate.T[None], grad_up.T[None], grad_down[None])


def solution(mesh):
    return jax.shard_map(
        per_device,
        mesh=mesh,
        in_specs=(
            P(("branch", "dp"), "mp"),
            P(("branch", "dp"), None),
            P("branch", "mp", "dp"),
            P(),
            P("branch", None, ("mp", "dp")),
            P("branch", None, ("mp", "dp")),
            P("branch", ("mp", "dp"), None),
            P(("branch", "dp"), None),
            P(("branch", "dp"), None),
            P(("branch", "dp"), None),
        ),
        out_specs=(
            P("branch", None, ("mp", "dp")),
            P("branch", None, ("mp", "dp")),
            P("branch", ("mp", "dp"), None),
        ),
        check_vma=False,
    )
```
